256 devices in a mesh: seq: 32 (over y_lo, z, core), head: 8 (over x, y_hi).
Axes of the slice: x: 4, y: 4 (y_hi: 2, y_lo: 2; y = y_hi * 2 + y_lo), z: 8, core: 2. Of those that a mesh axis runs over, the one named last changes fastest.
Arguments:
- queries: bfloat16 [4096, 128, 576], P('seq', 'head'), may hold values from -48 to 48
- latent_cache: bfloat16 [4096, 576], P('seq'), may hold values from -4 to 4
- grad_out: bfloat16 [4096, 128, 512], P('seq', 'head'), may hold values from -6 to 6
- segment_ids: int32 [4096], replicated, may hold values from 0 to 31, never falling along the last dimension, each value on 1 to 256 neighbouring positions
Outputs:
- grad_queries: bfloat16 [4096, 128, 576], P('seq', 'head')
- grad_cache: bfloat16 [4096, 576], P('seq')
The draws below stay inside these ranges and needn't reach their ends.
Inputs may be any that keep to these rules, and one draw needn't show every extreme that they name: `segment_ids`: document numbers never fall along the sequence; no document has more than 256 tokens and one has exactly 256.
All inputs are finite; a program needn't handle non-finite values.
Results may differ from the reference program's by a relative error of at most 0.0057.
Values may be sent and summed in bfloat16 or wider, within the bound.
A program may use at most 64 MiB of HBM per device.

```python
import math
import jax
import jax.numpy as jnp
import numpy as np
from jax import lax

HEADS = 128
LATENT = 512
KV = 576
TOK_DEV = 128
HOPS = 2
TOKENS = 4096
DOC_MOST = 256
SEGMENTS = 32
N_SEQ = 32


def base_cache(key):
    return jnp.clip(jax.random.normal(key, (TOKENS, KV), jnp.float32), -4.0, 4.0)


def draw_latent_cache(key, part):
    anchor = base_cache(key)
    return anchor.astype(jnp.bfloat16)


def draw_queries(key, part):
    key = jax.random.fold_in(key, 5)
    queries = jnp.clip(jax.random.normal(key, (TOKENS, HEADS, KV), jnp.float32), -4.0, 4.0)
    return queries.astype(jnp.bfloat16)


def shard_levels(rng, extent, cuts, least, largest):
    def one(axis_at, blocks):
        draws = jax.random.uniform(jax.random.fold_in(jax.random.fold_in(rng, 6), axis_at), (blocks,), jnp.float32, least / len(cuts), largest / len(cuts))
        return jnp.repeat(jnp.exp(draws), extent[axis_at] // blocks).reshape((-1,) + (1,) * (len(extent) - axis_at - 1))

    level = one(*cuts[0])
    for cut in cuts[1:]:
        level = level * one(*cut)
    return level


def profile(number_of, total, reach, lean):
    weights = [(1 << 20) // math.isqrt(standing ** lean) + 1 for standing in range(2, number_of + 1)]
    rest, counts = total - reach - (number_of - 1), [1] * (number_of - 1)
    while rest > 0:
        movable = [i for i in range(number_of - 1) if counts[i] < reach]
        mass, left = sum([weights[i] for i in movable]), rest
        for i in movable:
            addition = min(reach - counts[i], max(1, left * weights[i] // mass), rest)
            counts[i] = counts[i] + addition
            rest = rest - addition
    return np.array([reach] + counts)


def ragged(own_key, count, total, limit, lean):
    if count == 2:
        one = jax.random.randint(own_key, (), max(1, total - limit), min(limit, total - 1) + 1)
        return jnp.stack([one, total - one])
    sizes = jnp.asarray(profile(count, total, limit, lean), jnp.int32)
    couples = (count - 1) // 2
    donor, sink = sizes[1:1 + 2 * couples:2], sizes[2:2 + 2 * couples:2]
    room = jnp.minimum(donor - 1, limit - sink)
    passed = jax.random.randint(jax.random.fold_in(own_key, 1), (couples,), 0, 1 << 20) % (room + 1)
    sizes = sizes.at[1:1 + 2 * couples:2].set(donor - passed).at[2:2 + 2 * couples:2].set(sink + passed)
    return sizes[jax.random.permutation(jax.random.fold_in(own_key, 2), count)]


def bell_draw(key, extent, scale, reach, split=(), kind=jnp.bfloat16):
    loudness = shard_levels(key, extent, split, -0.22, 0.18) if split else 1.0
    array = jax.random.normal(key, extent, jnp.float32) * scale * loudness
    return jnp.minimum(jnp.maximum(array, -reach), reach).astype(kind)


def setup_inputs(seed: int = 0) -> dict:
    splits = jax.random.split(jax.random.key(seed), 5)
    queries = draw_queries(jax.random.fold_in(splits[4], 71), 0)
    latent_cache = draw_latent_cache(jax.random.fold_in(splits[4], 71), 0)
    grad_out = bell_draw(splits[2], (TOKENS, HEADS, LATENT), 1.0, 6.0, ((0, 32), (1, 8)))
    segment_ids = jnp.searchsorted(jnp.cumsum(ragged(splits[3], SEGMENTS, TOKENS, DOC_MOST, 2)), jnp.arange(TOKENS), side="right").astype(jnp.int32)
    return dict(queries=queries, latent_cache=latent_cache, grad_out=grad_out, segment_ids=segment_ids)


score_scale = 192.0 ** -0.5
masked_score = -1.0e30


def window_mask(segment_ids, block_index, block_rows, window_rows):
    seg_whole = segment_ids.astype(jnp.int32)
    filler = jnp.full((HOPS * block_rows,), -1, jnp.int32)
    padded = jnp.concatenate([filler, seg_whole])
    offset = (block_index * block_rows).astype(jnp.int32)
    query_seg = lax.dynamic_slice_in_dim(seg_whole, offset, block_rows)
    key_seg = lax.dynamic_slice_in_dim(padded, offset, window_rows)
    query_pos = lax.iota(jnp.int32, block_rows)[:, None] + HOPS * block_rows
    key_pos = lax.iota(jnp.int32, window_rows)[None, :]
    return (query_seg[:, None] == key_seg[None, :]) & (key_pos <= query_pos)


def reference(queries, latent_cache, grad_out, segment_ids):
    window_rows = (HOPS + 1) * TOK_DEV
    filler = jnp.zeros((HOPS * TOK_DEV, KV), latent_cache.dtype)
    padded_cache = jnp.concatenate([filler, latent_cache], axis=0)

    def one_block(carried, block_index):
        first_row = (block_index * TOK_DEV).astype(jnp.int32)
        block_queries = lax.dynamic_slice_in_dim(queries, first_row, TOK_DEV, 0).astype(jnp.float32)
        block_grads = lax.dynamic_slice_in_dim(grad_out, first_row, TOK_DEV, 0).astype(jnp.float32)
        window = lax.dynamic_slice_in_dim(padded_cache, first_row, window_rows, 0).astype(jnp.float32)
        values = window[:, :LATENT]
        visible = window_mask(segment_ids, block_index, TOK_DEV, window_rows)[None]
        scores = jnp.einsum("ihc,tc->hit", block_queries, window) * score_scale
        scores = jnp.where(visible, scores, masked_score)
        row_max = jnp.max(scores, axis=2, keepdims=True)
        expo_terms = jnp.where(visible, jnp.exp(scores - row_max), 0.0)
        weights = expo_terms / jnp.sum(expo_terms, axis=2, keepdims=True)
        weights_low = lax.optimization_barrier(weights.astype(jnp.bfloat16)).astype(jnp.float32)
        output = jnp.einsum("hit,tc->ihc", weights_low, values)
        row_delta = jnp.sum(block_grads * output, axis=2)
        grad_weights = jnp.einsum("ihc,tc->hit", block_grads, values)
        grad_scores = (score_scale * weights * (grad_weights - jnp.transpose(row_delta)[:, :, None])).astype(jnp.bfloat16)
        grad_scores = lax.optimization_barrier(grad_scores).astype(jnp.float32)
        grad_queries = jnp.einsum("hit,tc->ihc", grad_scores, window).astype(jnp.bfloat16)
        key_grad = jnp.einsum("hit,ihc->tc", grad_scores, block_queries)
        value_grad = jnp.einsum("hit,ihc->tc", weights_low, block_grads)
        key_grad = jnp.concatenate([key_grad[:, :LATENT] + value_grad, key_grad[:, LATENT:]], axis=1)
        previous = lax.dynamic_slice_in_dim(carried, first_row, window_rows, 0)
        carried = lax.dynamic_update_slice_in_dim(carried, previous + key_grad, first_row, 0)
        return carried, grad_queries

    initial = jnp.zeros((TOKENS + HOPS * TOK_DEV, KV), jnp.float32)
    carried, query_blocks = lax.scan(one_block, initial, jnp.arange(N_SEQ, dtype=jnp.int32))
    grad_cache = carried[HOPS * TOK_DEV:].astype(jnp.bfloat16)
    return query_blocks.reshape(TOKENS, HEADS, KV), grad_cache
```

```python
import functools

import jax
import jax.numpy as jnp
from jax import lax
from jax.experimental import pallas as pl
from jax.experimental.pallas import tpu as pltpu
from jax.sharding import PartitionSpec as P

MESH = pl.DeviceIdType.MESH
LATENT = 512
N_X = 4
score_scale = 192.0 ** (-0.5)
exp2_scale = score_scale * 1.4426950408889634
masked_score = -1e30
bf16 = jnp.bfloat16
f32 = jnp.float32


def dot(a, b):
    return lax.dot_general(a, b, (((1,), (0,)), ((), ())), preferred_element_type=f32)


def dot_nt(a, b):
    return lax.dot_general(a, b, (((1,), (1,)), ((), ())), preferred_element_type=f32)


def kernel(n_seq, n_head, q_hbm, kt_hbm, do_hbm, seg_hbm, dq_hbm, gc_ref,
           q, kt, kk, do, doh, dot_, seg, s0, g0, p_all, ds_all, dq, mask,
           psend, pown, rbuf, gbuf,
           lsem, osem, wsend, wrecv, psems, precv, gsend, grecv, ready):
    heads, kv, tok = q.shape
    pairs = heads // 2
    quarter = kv // N_X
    s = lax.axis_index("seq")
    h = lax.axis_index("head")
    x, y = h // 2, h % 2

    load_k = pltpu.make_async_copy(kt_hbm, kt.at[2], lsem.at[0])
    load_s = pltpu.make_async_copy(seg_hbm, seg, lsem.at[1])
    load_do = pltpu.make_async_copy(do_hbm, do, lsem.at[2])
    load_q = pltpu.make_async_copy(q_hbm, q, lsem.at[3])
    for c in (load_k, load_s, load_do, load_q):
        c.start()

    barrier = pltpu.get_barrier_semaphore()
    for d in (1, 2):
        @pl.when(s + d < n_seq)
        def _():
            pl.semaphore_signal(barrier, inc=1, device_id={"seq": s + d, "head": h}, device_id_type=MESH)

        @pl.when(s - d >= 0)
        def _():
            pl.semaphore_signal(barrier, inc=1, device_id={"seq": s - d, "head": h}, device_id_type=MESH)
    for d in range(1, n_head):
        pl.semaphore_signal(barrier, inc=1, device_id={"seq": s, "head": (h + d) % n_head}, device_id_type=MESH)
    ahead = jnp.minimum(n_seq - 1 - s, 2)
    behind = jnp.minimum(s, 2)
    pl.semaphore_wait(barrier, ahead + behind + n_head - 1)

    win = [
        pltpu.make_async_remote_copy(
            src_ref=kt_hbm, dst_ref=kt.at[2 - d], send_sem=wsend.at[d - 1], recv_sem=wrecv.at[d - 1],
            device_id={"seq": s + d, "head": h}, device_id_type=MESH)
        for d in (1, 2)
    ]
    for d in (1, 2):
        @pl.when(s + d < n_seq)
        def _():
            win[d - 1].start()

        @pl.when(s - d < 0)
        def _():
            kt[2 - d] = jnp.zeros((kv, tok), bf16)

        @pl.when(s + d >= n_seq)
        def _():
            for j in range(N_X):
                rbuf[(d - 1) * N_X + j] = jnp.zeros((quarter, tok), bf16)

    load_s.wait()
    row = lax.broadcasted_iota(jnp.int32, (tok, tok), 0)
    col = lax.broadcasted_iota(jnp.int32, (tok, tok), 1)
    tri = row <= col
    seg_q = jnp.broadcast_to(seg[pl.ds(s, 1), :], (tok, tok))

    def key_seg(d):
        line = jnp.broadcast_to(seg[pl.ds(jnp.maximum(s - d, 0), 1), :], (tok, tok))
        line = jnp.where(s - d >= 0, line, -1)
        return jnp.transpose(line)

    seen_p = jnp.where(tri, key_seg(0), key_seg(2)) == seg_q
    seen_1 = key_seg(1) == seg_q
    mask[0] = jnp.where(seen_1, 0.0, masked_score)
    mask[1] = jnp.where(seen_p, 0.0, masked_score)

    load_k.wait()
    kk[pl.ds(2 * tok, tok), :] = jnp.transpose(kt[2])
    load_do.wait()
    r = lax.broadcasted_iota(jnp.int32, (256, 256), 0)
    c = lax.broadcasted_iota(jnp.int32, (256, 256), 1)
    perm = ((r // 16 == c % 16) & (r % 16 == c // 16)).astype(bf16)
    for i in range(tok // 16):
        part = dot(perm, do[pl.ds(i * 256, 256), :]).astype(bf16)
        for hh in range(heads):
            doh[hh, pl.ds(i * 16, 16), :] = part[hh * 16:(hh + 1) * 16]
    for hh in range(heads):
        dot_[hh] = jnp.transpose(doh[hh])
    load_q.wait()

    def pair(ref, p):
        return jnp.concatenate([ref[2 * p], ref[2 * p + 1]], axis=1)

    for p in range(pairs):
        lanes = pl.ds(p * 256, 256)
        s0[:, lanes] = dot(kk[pl.ds(2 * tok, tok), :], pair(q, p))
        g0[:, lanes] = dot(kk[pl.ds(2 * tok, tok), :LATENT], pair(dot_, p))

    for d in (1, 2):
        @pl.when(s - d >= 0)
        def _():
            win[d - 1].wait_recv()
        kk[pl.ds((2 - d) * tok, tok), :] = jnp.transpose(kt[2 - d])
    for d in range(1, N_X):
        pl.semaphore_signal(ready, inc=1, device_id={"seq": s, "head": (h + 2 * d) % n_head}, device_id_type=MESH)

    tri2 = jnp.concatenate([tri, tri], axis=1)
    m1 = jnp.concatenate([mask[0], mask[0]], axis=1)
    mp = jnp.concatenate([mask[1], mask[1]], axis=1)
    for p in range(pairs):
        lanes = pl.ds(p * 256, 256)
        s12 = dot(kk[pl.ds(0, 2 * tok), :], pair(q, p))
        g12 = dot(kk[pl.ds(0, 2 * tok), :LATENT], pair(dot_, p))
        sp = jnp.where(tri2, s0[:, lanes], s12[:tok]) + mp
        s1 = s12[tok:] + m1
        top = jnp.maximum(jnp.max(sp, axis=0, keepdims=True), jnp.max(s1, axis=0, keepdims=True))
        ep = jnp.exp2((sp - top) * exp2_scale)
        e1 = jnp.exp2((s1 - top) * exp2_scale)
        inv = 1.0 / (jnp.sum(ep, axis=0, keepdims=True) + jnp.sum(e1, axis=0, keepdims=True))
        wp, w1 = ep * inv, e1 * inv
        wlp, wl1 = wp.astype(bf16), w1.astype(bf16)
        gp, g1 = jnp.where(tri2, g0[:, lanes], g12[:tok]), g12[tok:]
        delta = (jnp.sum(wlp.astype(f32) * gp, axis=0, keepdims=True)
                 + jnp.sum(wl1.astype(f32) * g1, axis=0, keepdims=True))
        dsp = (score_scale * wp * (gp - delta)).astype(bf16)
        ds1 = (score_scale * w1 * (g1 - delta)).astype(bf16)
        zero = jnp.zeros_like(wlp)
        p_all[0:tok, lanes] = jnp.where(tri2, zero, wlp)
        p_all[tok:2 * tok, lanes] = wl1
        p_all[2 * tok:, lanes] = jnp.where(tri2, wlp, zero)
        ds_all[0:tok, lanes] = jnp.where(tri2, zero, dsp)
        ds_all[tok:2 * tok, lanes] = ds1
        ds_all[2 * tok:, lanes] = jnp.where(tri2, dsp, zero)

    qall = jnp.concatenate([q[hh] for hh in range(heads)], axis=1)
    dall = jnp.concatenate([dot_[hh] for hh in range(heads)], axis=1)

    def key_grad(rows):
        from_keys = dot_nt(qall, ds_all[rows, :])
        from_values = dot_nt(dall, p_all[rows, :])
        return from_keys[:LATENT] + from_values, from_keys[LATENT:]

    low, high = key_grad(pl.ds(0, 2 * tok))
    for b in (0, 1):
        psend[b, :LATENT, :] = low[:, b * tok:(b + 1) * tok].astype(bf16)
        psend[b, LATENT:, :] = high[:, b * tok:(b + 1) * tok].astype(bf16)
    pl.semaphore_wait(ready, N_X - 1)

    def part_copy(b, j):
        xx = (x + j) % N_X
        slot = (1 - b) * N_X + j if b < 2 else 2 * N_X + j - 1
        return pltpu.make_async_remote_copy(
            src_ref=psend.at[b, pl.ds(pl.multiple_of(xx * quarter, 16), quarter)],
            dst_ref=rbuf.at[slot], send_sem=psems.at[slot], recv_sem=precv.at[slot],
            device_id={"seq": s - (2 - b), "head": xx * 2 + y}, device_id_type=MESH)

    for b in (0, 1):
        @pl.when(s >= 2 - b)
        def _():
            for j in (2, 1, 3, 0):
                part_copy(b, j).start()

    low, high = key_grad(pl.ds(2 * tok, tok))
    psend[2, :LATENT, :] = low.astype(bf16)
    psend[2, LATENT:, :] = high.astype(bf16)
    for j in (2, 1, 3):
        part_copy(2, j).start()
    pown[:LATENT, :] = low
    pown[LATENT:, :] = high

    ktall = jnp.concatenate([kt[0], kt[1], kt[2]], axis=1)
    for p in range(pairs):
        out = dot(ktall, ds_all[:, pl.ds(p * 256, 256)]).astype(bf16)
        dq[2 * p] = out[:, :tok]
        dq[2 * p + 1] = out[:, tok:]
    store = pltpu.make_async_copy(dq, dq_hbm, osem)
    store.start()

    total = pown[pl.ds(pl.multiple_of(x * quarter, 16), quarter), :]
    for b in (2, 1, 0):
        for j in range(1 if b == 2 else 0, N_X):
            if b == 2:
                part_copy(b, j).wait_recv()
            else:
                @pl.when(s + 2 - b < n_seq)
                def _():
                    part_copy(b, j).wait_recv()
            slot = (1 - b) * N_X + j if b < 2 else 2 * N_X + j - 1
            total = total + rbuf[slot].astype(f32)
    mine = pl.ds(pl.multiple_of(x * quarter, 16), quarter)
    gbuf[y, mine, :] = total.astype(bf16)

    def gather_copy(d):
        return pltpu.make_async_remote_copy(
            src_ref=gbuf.at[y, mine], dst_ref=gbuf.at[y, mine],
            send_sem=gsend.at[d - 1], recv_sem=grecv.at[d - 1],
            device_id={"seq": s, "head": (h + d) % n_head}, device_id_type=MESH)

    for d in (3, 5, 4, 1, 7, 2, 6):
        gather_copy(d).start()
    for d in (2, 6, 1, 7, 4, 3, 5):
        gather_copy(d).wait_recv()
    gc_ref[...] = (gbuf[0].astype(f32) + gbuf[1].astype(f32)).astype(bf16)

    for d in (1, 2):
        @pl.when(s + d < n_seq)
        def _():
            win[d - 1].wait_send()
    for b in (0, 1):
        @pl.when(s >= 2 - b)
        def _():
            for j in range(N_X):
                part_copy(b, j).wait_send()
    for j in range(1, N_X):
        part_copy(2, j).wait_send()
    for d in range(1, n_head):
        gather_copy(d).wait_send()
    store.wait()


def local(n_seq, n_head, queries, latent_cache, grad_out, segment_ids):
    tok, heads, kv = queries.shape
    q = jnp.transpose(queries, (1, 2, 0))
    kt = jnp.transpose(latent_cache)
    do = grad_out.reshape(tok * heads, LATENT)
    seg = segment_ids.reshape(n_seq, tok)
    rows = tok * heads
    quarter = kv // N_X
    dma = pltpu.SemaphoreType.DMA
    anywhere = pl.BlockSpec(memory_space=pl.ANY)
    dq, gc = pl.pallas_call(
        functools.partial(kernel, n_seq, n_head),
        out_shape=(jax.ShapeDtypeStruct((heads, kv, tok), bf16), jax.ShapeDtypeStruct((kv, tok), bf16)),
        in_specs=[anywhere] * 4,
        out_specs=(anywhere, pl.BlockSpec(memory_space=pltpu.VMEM)),
        scratch_shapes=[
            pltpu.VMEM((heads, kv, tok), bf16),
            pltpu.VMEM((3, kv, tok), bf16),
            pltpu.VMEM((3 * tok, kv), bf16),
            pltpu.VMEM((rows, LATENT), bf16),
            pltpu.VMEM((heads, tok, LATENT), bf16),
            pltpu.VMEM((heads, LATENT, tok), bf16),
            pltpu.VMEM((n_seq, tok), jnp.int32),
            pltpu.VMEM((tok, rows), f32),
            pltpu.VMEM((tok, rows), f32),
            pltpu.VMEM((3 * tok, rows), bf16),
            pltpu.VMEM((3 * tok, rows), bf16),
            pltpu.VMEM((heads, kv, tok), bf16),
            pltpu.VMEM((2, tok, tok), f32),
            pltpu.VMEM((3, kv, tok), bf16),
            pltpu.VMEM((kv, tok), f32),
            pltpu.VMEM((3 * N_X - 1, quarter, tok), bf16),
            pltpu.VMEM((2, kv, tok), bf16),
            dma((4,)), dma, dma((2,)), dma((2,)),
            dma((3 * N_X - 1,)), dma((3 * N_X - 1,)), dma((n_head - 1,)), dma((n_head - 1,)),
            pltpu.SemaphoreType.REGULAR,
        ],
        compiler_params=pltpu.CompilerParams(
            collective_id=0, has_side_effects=True, vmem_limit_bytes=50 << 20),
        cost_estimate=pl.CostEstimate(flops=6 * 10**9, bytes_accessed=8 * 10**6, transcendentals=10**6),
        name="latent_backward",
    )(q, kt, do, seg)
    return jnp.transpose(dq, (2, 0, 1)), jnp.transpose(gc)


def solution(mesh):
    in_specs = (P("seq", "head", None), P("seq", None), P("seq", "head", None), P())
    out_specs = (P("seq", "head", None), P("seq", None))
    return jax.shard_map(
        functools.partial(local, mesh.shape["seq"], mesh.shape["head"]),
        mesh=mesh, in_specs=in_specs, out_specs=out_specs, check_vma=False)
```

```python
import functools

import jax
import jax.numpy as jnp
from jax import lax
from jax.experimental import pallas as pl
from jax.experimental.pallas import tpu as pltpu
from jax.sharding import PartitionSpec as P

MESH = pl.DeviceIdType.MESH
LATENT = 512
N_X = 4
score_scale = 192.0 ** (-0.5)
exp2_scale = score_scale * 1.4426950408889634
masked_score = -1e30
bf16 = jnp.bfloat16
f32 = jnp.float32


def dot(a, b):
    return lax.dot_general(a, b, (((1,), (0,)), ((), ())), preferred_element_type=f32)


def dot_nt(a, b):
    return lax.dot_general(a, b, (((1,), (1,)), ((), ())), preferred_element_type=f32)


def kernel(n_seq, n_head, q_hbm, kt_hbm, do_hbm, seg_hbm, dq, gc_ref,
           q, kt, kk, do, doh, qn, dot_, seg, s0, g0, p_all, ds_all, mask,
           pmid, psend, pown, pacc, rbuf, gbuf,
           lsem, wsend, wrecv, msem, psems, precv, gsend, grecv, ready):
    heads, kv, tok = q.shape
    pairs = heads // 2
    quarter = kv // N_X
    s = lax.axis_index("seq")
    h = lax.axis_index("head")
    x, y = h // 2, h % 2
    core = s % 2

    load_k = pltpu.make_async_copy(kt_hbm, kt.at[2], lsem.at[0])
    load_s = pltpu.make_async_copy(seg_hbm, seg, lsem.at[1])
    load_do = pltpu.make_async_copy(do_hbm, do, lsem.at[2])
    load_q = pltpu.make_async_copy(q_hbm, q, lsem.at[3])
    load_k.start()
    load_s.start()

    barrier = pltpu.get_barrier_semaphore()
    for d in (1, 2):
        @pl.when(s + d < n_seq)
        def _():
            pl.semaphore_signal(barrier, inc=1, device_id={"seq": s + d, "head": h}, device_id_type=MESH)

        @pl.when(s - d >= 0)
        def _():
            pl.semaphore_signal(barrier, inc=1, device_id={"seq": s - d, "head": h}, device_id_type=MESH)
    for d in range(1, n_head):
        pl.semaphore_signal(barrier, inc=1, device_id={"seq": s, "head": (h + d) % n_head}, device_id_type=MESH)
    ahead = jnp.minimum(n_seq - 1 - s, 2)
    behind = jnp.minimum(s, 2)
    pl.semaphore_wait(barrier, ahead + behind + n_head - 1)

    win = [
        pltpu.make_async_remote_copy(
            src_ref=kt_hbm, dst_ref=kt.at[2 - d], send_sem=wsend.at[d - 1], recv_sem=wrecv.at[d - 1],
            device_id={"seq": s + d, "head": h}, device_id_type=MESH)
        for d in (1, 2)
    ]
    for d in (2, 1):
        @pl.when(s + d < n_seq)
        def _():
            win[d - 1].start()

        @pl.when(s - d < 0)
        def _():
            kt[2 - d] = jnp.zeros((kv, tok), bf16)

    @pl.when(s + 2 >= n_seq)
    def _():
        for j in range(N_X):
            rbuf[j] = jnp.zeros((quarter, tok), bf16)

    load_do.start()
    load_q.start()

    load_s.wait()
    row = lax.broadcasted_iota(jnp.int32, (tok, tok), 0)
    col = lax.broadcasted_iota(jnp.int32, (tok, tok), 1)
    tri = row <= col
    seg_q = jnp.broadcast_to(seg[pl.ds(s, 1), :], (tok, tok))

    def key_seg(d):
        line = jnp.broadcast_to(seg[pl.ds(jnp.maximum(s - d, 0), 1), :], (tok, tok))
        line = jnp.where(s - d >= 0, line, -1)
        return jnp.transpose(line)

    seen_p = jnp.where(tri, key_seg(0), key_seg(2)) == seg_q
    seen_1 = key_seg(1) == seg_q
    mask[0] = jnp.where(seen_1, 0.0, masked_score)
    mask[1] = jnp.where(seen_p, 0.0, masked_score)

    load_k.wait()
    kk[pl.ds(2 * tok, tok), :] = jnp.transpose(kt[2])
    load_do.wait()
    r = lax.broadcasted_iota(jnp.int32, (256, 256), 0)
    c = lax.broadcasted_iota(jnp.int32, (256, 256), 1)
    perm = ((r // 16 == c % 16) & (r % 16 == c // 16)).astype(bf16)
    for i in range(tok // 16):
        part = dot(perm, do[pl.ds(i * 256, 256), :]).astype(bf16)
        for hh in range(heads):
            doh[pl.ds(hh * tok + i * 16, 16), :] = part[hh * 16:(hh + 1) * 16]
    for hh in range(heads):
        dot_[hh] = jnp.transpose(doh[pl.ds(hh * tok, tok), :])
    load_q.wait()

    def pair(ref, p):
        return jnp.concatenate([ref[2 * p], ref[2 * p + 1]], axis=1)

    for p in range(pairs):
        lanes = pl.ds(p * 256, 256)
        s0[:, lanes] = dot(kk[pl.ds(2 * tok, tok), :], pair(q, p))
        g0[:, lanes] = dot(kk[pl.ds(2 * tok, tok), :LATENT], pair(dot_, p))

    for hh in range(heads):
        qn[pl.ds(hh * tok, tok), :] = jnp.transpose(q[hh])

    for d in (1, 2):
        @pl.when(s - d >= 0)
        def _():
            win[d - 1].wait_recv()
        kk[pl.ds((2 - d) * tok, tok), :] = jnp.transpose(kt[2 - d])
    for d in range(1, N_X):
        pl.semaphore_signal(ready, inc=1, device_id={"seq": s, "head": (h + 2 * d) % n_head}, device_id_type=MESH)

    tri2 = jnp.concatenate([tri, tri], axis=1)
    m1 = jnp.concatenate([mask[0], mask[0]], axis=1)
    mp = jnp.concatenate([mask[1], mask[1]], axis=1)
    for p in range(pairs):
        lanes = pl.ds(p * 256, 256)
        s12 = dot(kk[pl.ds(0, 2 * tok), :], pair(q, p))
        g12 = dot(kk[pl.ds(0, 2 * tok), :LATENT], pair(dot_, p))
        sp = jnp.where(tri2, s0[:, lanes], s12[:tok]) + mp
        s1 = s12[tok:] + m1
        top = jnp.maximum(jnp.max(sp, axis=0, keepdims=True), jnp.max(s1, axis=0, keepdims=True))
        ep = jnp.exp2((sp - top) * exp2_scale)
        e1 = jnp.exp2((s1 - top) * exp2_scale)
        inv = 1.0 / (jnp.sum(ep, axis=0, keepdims=True) + jnp.sum(e1, axis=0, keepdims=True))
        wp, w1 = ep * inv, e1 * inv
        wlp, wl1 = wp.astype(bf16), w1.astype(bf16)
        gp, g1 = jnp.where(tri2, g0[:, lanes], g12[:tok]), g12[tok:]
        delta = (jnp.sum(wlp.astype(f32) * gp, axis=0, keepdims=True)
                 + jnp.sum(wl1.astype(f32) * g1, axis=0, keepdims=True))
        dsp = (score_scale * wp * (gp - delta)).astype(bf16)
        ds1 = (score_scale * w1 * (g1 - delta)).astype(bf16)
        zero = jnp.zeros_like(wlp)
        p_all[0:tok, lanes] = jnp.where(tri2, zero, wlp)
        p_all[tok:2 * tok, lanes] = wl1
        p_all[2 * tok:, lanes] = jnp.where(tri2, wlp, zero)
        ds_all[0:tok, lanes] = jnp.where(tri2, zero, dsp)
        ds_all[tok:2 * tok, lanes] = ds1
        ds_all[2 * tok:, lanes] = jnp.where(tri2, dsp, zero)

    def key_grad(block):
        rows = pl.ds(block * tok, tok)
        pown[...] = dot(ds_all[rows, :], qn[...])
        pown[:, :LATENT] += dot(p_all[rows, :], doh[...])
        return pown[...]

    swap = pltpu.make_async_remote_copy(
        src_ref=pmid.at[0], dst_ref=pmid.at[1], send_sem=msem.at[0], recv_sem=msem.at[1],
        device_id={"seq": s + 1 - 2 * core, "head": h}, device_id_type=MESH)

    def part_copy(b, j):
        xx = (x + j) % N_X
        slot = b * N_X + j - b
        return pltpu.make_async_remote_copy(
            src_ref=psend.at[b, pl.ds(pl.multiple_of(xx * quarter, 16), quarter)],
            dst_ref=rbuf.at[slot], send_sem=psems.at[slot], recv_sem=precv.at[slot],
            device_id={"seq": s - 2 * (1 - b), "head": xx * 2 + y}, device_id_type=MESH)

    def middle():
        pmid[0] = key_grad(1).astype(bf16)

        @pl.when(s > 0)
        def _():
            swap.start()

    @pl.when(core == 0)
    def _():
        pacc[...] = key_grad(2)
        middle()
        swap.wait_recv()
        psend[1] = jnp.transpose((pacc[...] + pmid[1].astype(f32)).astype(bf16))

    @pl.when(core == 1)
    def _():
        middle()
        psend[1] = jnp.transpose(key_grad(2).astype(bf16))

    pl.semaphore_wait(ready, N_X - 1)
    for j in (2, 1, 3):
        part_copy(1, j).start()

    @pl.when(s >= 2)
    def _():
        key_grad(0)

        @pl.when(core == 1)
        def _():
            swap.wait_recv()
            pown[...] += pmid[1].astype(f32)
        psend[0] = jnp.transpose(pown[...].astype(bf16))
        for j in (2, 1, 3, 0):
            part_copy(0, j).start()

    ktall = jnp.concatenate([kt[0], kt[1], kt[2]], axis=1)
    for p in range(pairs):
        out = dot(ktall, ds_all[:, pl.ds(p * 256, 256)]).astype(bf16)
        dq[2 * p] = out[:, :tok]
        dq[2 * p + 1] = out[:, tok:]


    total = psend[1, pl.ds(pl.multiple_of(x * quarter, 16), quarter), :].astype(f32)
    for j in range(1, N_X):
        part_copy(1, j).wait_recv()
        total = total + rbuf[N_X + j - 1].astype(f32)
    for j in range(N_X):
        @pl.when(s + 2 < n_seq)
        def _():
            part_copy(0, j).wait_recv()
        total = total + rbuf[j].astype(f32)
    mine = pl.ds(pl.multiple_of(x * quarter, 16), quarter)
    gbuf[y, mine, :] = total.astype(bf16)

    def gather_copy(d):
        return pltpu.make_async_remote_copy(
            src_ref=gbuf.at[y, mine], dst_ref=gbuf.at[y, mine],
            send_sem=gsend.at[d - 1], recv_sem=grecv.at[d - 1],
            device_id={"seq": s, "head": (h + d) % n_head}, device_id_type=MESH)

    for d in (3, 5, 4, 1, 7, 2, 6):
        gather_copy(d).start()
    for d in (2, 6, 1, 7, 4, 3, 5):
        gather_copy(d).wait_recv()
    gc_ref[...] = (gbuf[0].astype(f32) + gbuf[1].astype(f32)).astype(bf16)

    for d in (1, 2):
        @pl.when(s + d < n_seq)
        def _():
            win[d - 1].wait_send()
    @pl.when(s > 0)
    def _():
        swap.wait_send()

    @pl.when(s >= 2)
    def _():
        for j in range(N_X):
            part_copy(0, j).wait_send()
    for j in range(1, N_X):
        part_copy(1, j).wait_send()
    for d in range(1, n_head):
        gather_copy(d).wait_send()


def store_kernel(dq, gc, dq_hbm, gc_hbm, sems):
    copies = [pltpu.make_async_copy(gc, gc_hbm, sems.at[0]), pltpu.make_async_copy(dq, dq_hbm, sems.at[1])]
    for c in copies:
        c.start()
    for c in copies:
        c.wait()


def local(n_seq, n_head, queries, latent_cache, grad_out, segment_ids):
    tok, heads, kv = queries.shape
    q = jnp.transpose(queries, (1, 2, 0))
    kt = jnp.transpose(latent_cache)
    do = grad_out.reshape(tok * heads, LATENT)
    seg = segment_ids.reshape(n_seq, tok)
    rows = tok * heads
    quarter = kv // N_X
    dma = pltpu.SemaphoreType.DMA
    hbm = pl.BlockSpec(memory_space=pltpu.HBM)
    dq, gc = pl.pallas_call(
        functools.partial(kernel, n_seq, n_head),
        out_shape=(pltpu.VMEM((heads, kv, tok), bf16), pltpu.VMEM((kv, tok), bf16)),
        in_specs=[hbm] * 4,
        out_specs=(pl.BlockSpec(memory_space=pltpu.VMEM), pl.BlockSpec(memory_space=pltpu.VMEM)),
        scratch_shapes=[
            pltpu.VMEM((heads, kv, tok), bf16),
            pltpu.VMEM((3, kv, tok), bf16),
            pltpu.VMEM((3 * tok, kv), bf16),
            pltpu.VMEM((rows, LATENT), bf16),
            pltpu.VMEM((rows, LATENT), bf16),
            pltpu.VMEM((rows, kv), bf16),
            pltpu.VMEM((heads, LATENT, tok), bf16),
            pltpu.VMEM((n_seq, tok), jnp.int32),
            pltpu.VMEM((tok, rows), f32),
            pltpu.VMEM((tok, rows), f32),
            pltpu.VMEM((3 * tok, rows), bf16),
            pltpu.VMEM((3 * tok, rows), bf16),
            pltpu.VMEM((2, tok, tok), f32),
            pltpu.VMEM((2, tok, kv), bf16),
            pltpu.VMEM((2, kv, tok), bf16),
            pltpu.VMEM((tok, kv), f32),
            pltpu.VMEM((tok, kv), f32),
            pltpu.VMEM((2 * N_X - 1, quarter, tok), bf16),
            pltpu.VMEM((2, kv, tok), bf16),
            dma((4,)), dma((2,)), dma((2,)), dma((2,)),
            dma((2 * N_X - 1,)), dma((2 * N_X - 1,)), dma((n_head - 1,)), dma((n_head - 1,)),
            pltpu.SemaphoreType.REGULAR,
        ],
        compiler_params=pltpu.CompilerParams(
            collective_id=0, has_side_effects=True, vmem_limit_bytes=50 << 20),
        cost_estimate=pl.CostEstimate(flops=6 * 10**9, bytes_accessed=8 * 10**6, transcendentals=10**6),
        name="latent_backward",
    )(*[pltpu.with_memory_space_constraint(a, pltpu.HBM) for a in (q, kt, do, seg)])
    dq, gc = pl.pallas_call(
        store_kernel,
        out_shape=(jax.ShapeDtypeStruct((heads, kv, tok), bf16), jax.ShapeDtypeStruct((kv, tok), bf16)),
        in_specs=[pl.BlockSpec(memory_space=pltpu.VMEM)] * 2,
        out_specs=(hbm, hbm),
        scratch_shapes=[dma((2,))],
        name="store",
    )(*[pltpu.with_memory_space_constraint(a, pltpu.VMEM) for a in (dq, gc)])
    return jnp.transpose(dq, (2, 0, 1)), jnp.transpose(gc)


def solution(mesh):
    in_specs = (P("seq", "head", None), P("seq", None), P("seq", "head", None), P())
    out_specs = (P("seq", "head", None), P("seq", None))
    return jax.shard_map(
        functools.partial(local, mesh.shape["seq"], mesh.shape["head"]),
        mesh=mesh, in_specs=in_specs, out_specs=out_specs, check_vma=False)
```

```python
import functools

import jax
import jax.numpy as jnp
from jax import lax
from jax.experimental import pallas as pl
from jax.experimental.pallas import tpu as pltpu
from jax.sharding import PartitionSpec as P

MESH = pl.DeviceIdType.MESH
LATENT = 512
N_X = 4
score_scale = 192.0 ** (-0.5)
exp2_scale = score_scale * 1.4426950408889634
masked_score = -1e30
bf16 = jnp.bfloat16
f32 = jnp.float32


def dot(a, b):
    return lax.dot_general(a, b, (((1,), (0,)), ((), ())), preferred_element_type=f32)


def dot_nt(a, b):
    return lax.dot_general(a, b, (((1,), (1,)), ((), ())), preferred_element_type=f32)


def kernel(n_seq, n_head, q_hbm, kt_hbm, do_hbm, seg_hbm, dq, gc_ref,
           q, kt, kk, do, doh, qn, dot_, seg, s0, g0, sx, gx, p_all, ds_all, mask,
           pmid, psend, pown, rbuf, gbuf,
           lsem, wsend, wrecv, msem, psems, precv, gsend, grecv, here, ready):
    heads, kv, tok = q.shape
    pairs = heads // 2
    quarter = kv // N_X
    s = lax.axis_index("seq")
    h = lax.axis_index("head")
    x, y = h // 2, h % 2
    core = s % 2

    load_k = pltpu.make_async_copy(kt_hbm, kt.at[2], lsem.at[0])
    load_s = pltpu.make_async_copy(seg_hbm, seg, lsem.at[1])
    load_do = pltpu.make_async_copy(do_hbm, do, lsem.at[2])
    load_q = pltpu.make_async_copy(q_hbm, q, lsem.at[3])
    load_k.start()
    load_s.start()

    barrier = pltpu.get_barrier_semaphore()
    @pl.when(s + 2 < n_seq)
    def _():
        pl.semaphore_signal(barrier, inc=1, device_id={"seq": s + 2, "head": h}, device_id_type=MESH)

    @pl.when(s >= 2)
    def _():
        pl.semaphore_signal(barrier, inc=1, device_id={"seq": s - 2, "head": h}, device_id_type=MESH)
    pl.semaphore_signal(barrier, inc=1, device_id={"seq": s + 1 - 2 * core, "head": h}, device_id_type=MESH)

    def tell_heads(sem):
        for d in range(1, n_head):
            pl.semaphore_signal(sem, inc=1, device_id={"seq": s, "head": (h + d) % n_head}, device_id_type=MESH)

    @pl.when(h == 0)
    def _():
        tell_heads(barrier)
    ends = (s < 2).astype(jnp.int32) + (s + 2 >= n_seq).astype(jnp.int32)
    load_k.wait()
    pl.semaphore_wait(barrier, 3 - ends + (h > 0).astype(jnp.int32))

    half = kv // 2

    def win_copy(slot, i):
        part = pl.ds(i * half, half)
        if slot == 0:
            src, to = kt.at[2], s + 2
        else:
            src, to = kt.at[0], s + 1 - 2 * core
        return pltpu.make_async_remote_copy(
            src_ref=src.at[part], dst_ref=kt.at[slot, part], send_sem=wsend.at[2 * slot + i],
            recv_sem=wrecv.at[2 * slot + i], device_id={"seq": to, "head": h}, device_id_type=MESH)

    def own_copy(i):
        part = pl.ds(i * half, half)
        return pltpu.make_async_remote_copy(
            src_ref=kt.at[2, part], dst_ref=kt.at[1, part], send_sem=wsend.at[2 + i],
            recv_sem=wrecv.at[2 + i], device_id={"seq": s + 1, "head": h}, device_id_type=MESH)

    @pl.when(s + 2 < n_seq)
    def _():
        for i in (0, 1):
            win_copy(0, i).start()

    @pl.when(core == 0)
    def _():
        for i in (0, 1):
            own_copy(i).start()

    @pl.when(s < 2)
    def _():
        kt[0] = jnp.zeros((kv, tok), bf16)

    @pl.when(s == 0)
    def _():
        kt[1] = jnp.zeros((kv, tok), bf16)

    @pl.when(s + 2 >= n_seq)
    def _():
        for j in range(N_X):
            rbuf[j] = jnp.zeros((quarter, tok), bf16)

    load_do.start()
    load_q.start()

    @pl.when(h > 0)
    def _():
        pl.semaphore_signal(here, inc=1, device_id={"seq": s, "head": 0}, device_id_type=MESH)

    load_s.wait()
    row = lax.broadcasted_iota(jnp.int32, (tok, tok), 0)
    col = lax.broadcasted_iota(jnp.int32, (tok, tok), 1)
    tri = row <= col
    seg_q = jnp.broadcast_to(seg[pl.ds(s, 1), :], (tok, tok))

    def key_seg(d):
        line = jnp.broadcast_to(seg[pl.ds(jnp.maximum(s - d, 0), 1), :], (tok, tok))
        line = jnp.where(s - d >= 0, line, -1)
        return jnp.transpose(line)

    seen_p = jnp.where(tri, key_seg(0), key_seg(2)) == seg_q
    seen_1 = key_seg(1) == seg_q
    mask[0] = jnp.where(seen_1, 0.0, masked_score)
    mask[1] = jnp.where(seen_p, 0.0, masked_score)

    kk[pl.ds(2 * tok, tok), :] = jnp.transpose(kt[2])
    load_do.wait()
    r = lax.broadcasted_iota(jnp.int32, (256, 256), 0)
    c = lax.broadcasted_iota(jnp.int32, (256, 256), 1)
    perm = ((r // 16 == c % 16) & (r % 16 == c // 16)).astype(bf16)
    for i in range(tok // 16):
        part = dot(perm, do[pl.ds(i * 256, 256), :]).astype(bf16)
        for hh in range(heads):
            doh[pl.ds(hh * tok + i * 16, 16), :] = part[hh * 16:(hh + 1) * 16]
    for hh in range(heads):
        dot_[hh] = jnp.transpose(doh[pl.ds(hh * tok, tok), :])
    load_q.wait()

    def pair(ref, p):
        return jnp.concatenate([ref[2 * p], ref[2 * p + 1]], axis=1)

    for p in range(pairs):
        lanes = pl.ds(p * 256, 256)
        s0[:, lanes] = dot(kk[pl.ds(2 * tok, tok), :], pair(q, p))
        g0[:, lanes] = dot(kk[pl.ds(2 * tok, tok), :LATENT], pair(dot_, p))

    @pl.when(h == 0)
    def _():
        pl.semaphore_wait(here, n_head - 1)
        tell_heads(here)

    for hh in range(heads):
        qn[pl.ds(hh * tok, tok), :] = jnp.transpose(q[hh])

    @pl.when(h > 0)
    def _():
        pl.semaphore_wait(here, 1)

    tri2 = jnp.concatenate([tri, tri], axis=1)
    m1 = jnp.concatenate([mask[0], mask[0]], axis=1)
    mp = jnp.concatenate([mask[1], mask[1]], axis=1)

    def first(slot):
        rows = pl.ds(slot * tok, tok)
        kk[rows, :] = jnp.transpose(kt[slot])
        for p in range(pairs):
            lanes = pl.ds(p * 256, 256)
            sx[:, lanes] = dot(kk[rows, :], pair(q, p))
            gx[:, lanes] = dot(kk[rows, :LATENT], pair(dot_, p))

    def second(slot):
        rows = pl.ds(slot * tok, tok)
        kk[rows, :] = jnp.transpose(kt[slot])
        for p in range(pairs):
            lanes = pl.ds(p * 256, 256)
            sy = dot(kk[rows, :], pair(q, p))
            gy = dot(kk[rows, :LATENT], pair(dot_, p))
            s1, s2 = (sy, sx[:, lanes]) if slot == 1 else (sx[:, lanes], sy)
            g1, g2 = (gy, gx[:, lanes]) if slot == 1 else (gx[:, lanes], gy)
            weigh(lanes, s1, s2, g1, g2)

    def weigh(lanes, s1, s2, g1, g2):
        sp = jnp.where(tri2, s0[:, lanes], s2) + mp
        s1 = s1 + m1
        top = jnp.maximum(jnp.max(sp, axis=0, keepdims=True), jnp.max(s1, axis=0, keepdims=True))
        ep = jnp.exp2((sp - top) * exp2_scale)
        e1 = jnp.exp2((s1 - top) * exp2_scale)
        inv = 1.0 / (jnp.sum(ep, axis=0, keepdims=True) + jnp.sum(e1, axis=0, keepdims=True))
        wp, w1 = ep * inv, e1 * inv
        wlp, wl1 = wp.astype(bf16), w1.astype(bf16)
        gp = jnp.where(tri2, g0[:, lanes], g2)
        delta = (jnp.sum(wlp.astype(f32) * gp, axis=0, keepdims=True)
                 + jnp.sum(wl1.astype(f32) * g1, axis=0, keepdims=True))
        dsp = (score_scale * wp * (gp - delta)).astype(bf16)
        ds1 = (score_scale * w1 * (g1 - delta)).astype(bf16)
        zero = jnp.zeros_like(wlp)
        p_all[tok:2 * tok, lanes] = jnp.where(tri2, zero, wlp)
        p_all[0:tok, lanes] = wl1
        p_all[2 * tok:, lanes] = jnp.where(tri2, wlp, zero)
        ds_all[tok:2 * tok, lanes] = jnp.where(tri2, zero, dsp)
        ds_all[0:tok, lanes] = ds1
        ds_all[2 * tok:, lanes] = jnp.where(tri2, dsp, zero)

    def tell():
        for d in range(1, N_X):
            pl.semaphore_signal(ready, inc=1, device_id={"seq": s, "head": (h + 2 * d) % n_head}, device_id_type=MESH)

    @pl.when(core == 0)
    def _():
        @pl.when(s >= 2)
        def _():
            for i in (0, 1):
                win_copy(0, i).wait_recv()
        tell()
        first(0)

        @pl.when(s >= 2)
        def _():
            for i in (0, 1):
                win_copy(1, i).wait_recv()
        second(1)

    @pl.when(core == 1)
    def _():
        for i in (0, 1):
            win_copy(1, i).wait_recv()
        first(1)

        @pl.when(s >= 2)
        def _():
            for i in (0, 1):
                win_copy(0, i).wait_recv()
                win_copy(1, i).start()
        tell()
        second(0)

    def key_grad(rows):
        from_keys = dot(ds_all[rows, :], qn[...])
        return from_keys[:, :LATENT] + dot(p_all[rows, :], doh[...]), from_keys[:, LATENT:]

    swap = pltpu.make_async_remote_copy(
        src_ref=pmid.at[0], dst_ref=pmid.at[1], send_sem=msem.at[0], recv_sem=msem.at[1],
        device_id={"seq": s + 1 - 2 * core, "head": h}, device_id_type=MESH)

    def part_copy(b, j):
        xx = (x + j) % N_X
        slot = b * N_X + j - b
        return pltpu.make_async_remote_copy(
            src_ref=psend.at[b, pl.ds(pl.multiple_of(xx * quarter, 16), quarter)],
            dst_ref=rbuf.at[slot], send_sem=psems.at[slot], recv_sem=precv.at[slot],
            device_id={"seq": s - 2 * (1 - b), "head": xx * 2 + y}, device_id_type=MESH)

    low, high = key_grad(pl.ds(0, tok))
    pmid[0, :, :LATENT] = low.astype(bf16)
    pmid[0, :, LATENT:] = high.astype(bf16)

    @pl.when(s > 0)
    def _():
        swap.start()
    low, high = key_grad(pl.ds(tok, 2 * tok))
    pown[:, :LATENT] = low
    pown[:, LATENT:] = high
    pl.semaphore_wait(ready, N_X - 1)

    def emit(b, add):
        rows = pl.ds(b * tok, tok)
        if add:
            swap.wait_recv()
            psend[b] = jnp.transpose((pown[rows, :] + pmid[1].astype(f32)).astype(bf16))
        else:
            psend[b] = jnp.transpose(pown[rows, :].astype(bf16))
        if b == 0:
            @pl.when(s >= 2)
            def _():
                for j in (2, 1, 3, 0):
                    part_copy(0, j).start()
        else:
            for j in (2, 1, 3):
                part_copy(1, j).start()

    @pl.when(core == 0)
    def _():
        emit(0, False)
        emit(1, True)

    @pl.when((core == 1) & (s >= 2))
    def _():
        emit(0, True)

    @pl.when(core == 1)
    def _():
        emit(1, False)

    ktall = jnp.concatenate([kt[1], kt[0], kt[2]], axis=1)
    for p in range(pairs):
        out = dot(ktall, ds_all[:, pl.ds(p * 256, 256)]).astype(bf16)
        dq[2 * p] = out[:, :tok]
        dq[2 * p + 1] = out[:, tok:]


    total = psend[1, pl.ds(pl.multiple_of(x * quarter, 16), quarter), :].astype(f32)
    for j in range(1, N_X):
        part_copy(1, j).wait_recv()
        total = total + rbuf[N_X + j - 1].astype(f32)
    for j in range(N_X):
        @pl.when(s + 2 < n_seq)
        def _():
            part_copy(0, j).wait_recv()
        total = total + rbuf[j].astype(f32)
    mine = pl.ds(pl.multiple_of(x * quarter, 16), quarter)
    gbuf[y, mine, :] = total.astype(bf16)

    def gather_copy(d):
        return pltpu.make_async_remote_copy(
            src_ref=gbuf.at[y, mine], dst_ref=gbuf.at[y, mine],
            send_sem=gsend.at[d - 1], recv_sem=grecv.at[d - 1],
            device_id={"seq": s, "head": (h + d) % n_head}, device_id_type=MESH)

    for d in (3, 5, 4, 1, 7, 2, 6):
        gather_copy(d).start()
    for d in (2, 6, 1, 7, 4, 3, 5):
        gather_copy(d).wait_recv()
    gc_ref[...] = (gbuf[0].astype(f32) + gbuf[1].astype(f32)).astype(bf16)

    @pl.when(s + 2 < n_seq)
    def _():
        for i in (0, 1):
            win_copy(0, i).wait_send()

    @pl.when((core == 0) | (s >= 2))
    def _():
        for i in (0, 1):
            win_copy(1, i).wait_send()

    @pl.when(s > 0)
    def _():
        swap.wait_send()

    @pl.when(s >= 2)
    def _():
        for j in range(N_X):
            part_copy(0, j).wait_send()
    for j in range(1, N_X):
        part_copy(1, j).wait_send()
    for d in range(1, n_head):
        gather_copy(d).wait_send()


def store_kernel(dq, gc, dq_hbm, gc_hbm, sems):
    copies = [pltpu.make_async_copy(gc, gc_hbm, sems.at[0]), pltpu.make_async_copy(dq, dq_hbm, sems.at[1])]
    for c in copies:
        c.start()
    for c in copies:
        c.wait()


def local(n_seq, n_head, queries, latent_cache, grad_out, segment_ids):
    tok, heads, kv = queries.shape
    q = jnp.transpose(queries, (1, 2, 0))
    kt = jnp.transpose(latent_cache)
    do = grad_out.reshape(tok * heads, LATENT)
    seg = segment_ids.reshape(n_seq, tok)
    rows = tok * heads
    quarter = kv // N_X
    dma = pltpu.SemaphoreType.DMA
    hbm = pl.BlockSpec(memory_space=pltpu.HBM)
    dq, gc = pl.pallas_call(
        functools.partial(kernel, n_seq, n_head),
        out_shape=(pltpu.VMEM((heads, kv, tok), bf16), pltpu.VMEM((kv, tok), bf16)),
        in_specs=[hbm] * 4,
        out_specs=(pl.BlockSpec(memory_space=pltpu.VMEM), pl.BlockSpec(memory_space=pltpu.VMEM)),
        scratch_shapes=[
            pltpu.VMEM((heads, kv, tok), bf16),
            pltpu.VMEM((3, kv, tok), bf16),
            pltpu.VMEM((3 * tok, kv), bf16),
            pltpu.VMEM((rows, LATENT), bf16),
            pltpu.VMEM((rows, LATENT), bf16),
            pltpu.VMEM((rows, kv), bf16),
            pltpu.VMEM((heads, LATENT, tok), bf16),
            pltpu.VMEM((n_seq, tok), jnp.int32),
            pltpu.VMEM((tok, rows), f32),
            pltpu.VMEM((tok, rows), f32),
            pltpu.VMEM((tok, rows), f32),
            pltpu.VMEM((tok, rows), f32),
            pltpu.VMEM((3 * tok, rows), bf16),
            pltpu.VMEM((3 * tok, rows), bf16),
            pltpu.VMEM((2, tok, tok), f32),
            pltpu.VMEM((2, tok, kv), bf16),
            pltpu.VMEM((2, kv, tok), bf16),
            pltpu.VMEM((2 * tok, kv), f32),
            pltpu.VMEM((2 * N_X - 1, quarter, tok), bf16),
            pltpu.VMEM((2, kv, tok), bf16),
            dma((4,)), dma((4,)), dma((4,)), dma((2,)),
            dma((2 * N_X - 1,)), dma((2 * N_X - 1,)), dma((n_head - 1,)), dma((n_head - 1,)),
            pltpu.SemaphoreType.REGULAR,
            pltpu.SemaphoreType.REGULAR,
        ],
        compiler_params=pltpu.CompilerParams(
            collective_id=0, has_side_effects=True, vmem_limit_bytes=50 << 20),
        cost_estimate=pl.CostEstimate(flops=6 * 10**9, bytes_accessed=8 * 10**6, transcendentals=10**6),
        name="latent_backward",
    )(*[pltpu.with_memory_space_constraint(a, pltpu.HBM) for a in (q, kt, do, seg)])
    dq, gc = pl.pallas_call(
        store_kernel,
        out_shape=(jax.ShapeDtypeStruct((heads, kv, tok), bf16), jax.ShapeDtypeStruct((kv, tok), bf16)),
        in_specs=[pl.BlockSpec(memory_space=pltpu.VMEM)] * 2,
        out_specs=(hbm, hbm),
        scratch_shapes=[dma((2,))],
        name="store",
    )(*[pltpu.with_memory_space_constraint(a, pltpu.VMEM) for a in (dq, gc)])
    return jnp.transpose(dq, (2, 0, 1)), jnp.transpose(gc)


def solution(mesh):
    in_specs = (P("seq", "head", None), P("seq", None), P("seq", "head", None), P())
    out_specs = (P("seq", "head", None), P("seq", None))
    return jax.shard_map(
        functools.partial(local, mesh.shape["seq"], mesh.shape["head"]),
        mesh=mesh, in_specs=in_specs, out_specs=out_specs, check_vma=False)
```

```python
import functools

import jax
import jax.numpy as jnp
from jax import lax
from jax.experimental import pallas as pl
from jax.experimental.pallas import tpu as pltpu
from jax.sharding import PartitionSpec as P

MESH = pl.DeviceIdType.MESH
LATENT = 512
N_X = 4
score_scale = 192.0 ** (-0.5)
exp2_scale = score_scale * 1.4426950408889634
masked_score = -1e30
bf16 = jnp.bfloat16
f32 = jnp.float32


def dot(a, b):
    return lax.dot_general(a, b, (((1,), (0,)), ((), ())), preferred_element_type=f32)


def dot_nt(a, b):
    return lax.dot_general(a, b, (((1,), (1,)), ((), ())), preferred_element_type=f32)


def kernel(n_seq, n_head, q_hbm, kt_hbm, do_hbm, seg_hbm, dq, gc_ref,
           q, kt, kk, do, doh, qn, dot_, seg, s0, g0, sx, gx, p_all, ds_all, mask,
           pmid, psend, pown, rbuf, gbuf,
           lsem, wsend, wrecv, msem, psems, precv, gsend, grecv, here, ready):
    heads, kv, tok = q.shape
    pairs = heads // 2
    quarter = kv // N_X
    s = lax.axis_index("seq")
    h = lax.axis_index("head")
    x, y = h // 2, h % 2
    core = s % 2

    load_k = pltpu.make_async_copy(kt_hbm, kt.at[2], lsem.at[0])
    load_s = pltpu.make_async_copy(seg_hbm, seg, lsem.at[1])
    load_do = pltpu.make_async_copy(do_hbm, do, lsem.at[2])
    load_q = pltpu.make_async_copy(q_hbm, q, lsem.at[3])
    load_k.start()
    load_s.start()

    barrier = pltpu.get_barrier_semaphore()
    @pl.when(s + 2 < n_seq)
    def _():
        pl.semaphore_signal(barrier, inc=1, device_id={"seq": s + 2, "head": h}, device_id_type=MESH)

    @pl.when(s >= 2)
    def _():
        pl.semaphore_signal(barrier, inc=1, device_id={"seq": s - 2, "head": h}, device_id_type=MESH)
    pl.semaphore_signal(barrier, inc=1, device_id={"seq": s + 1 - 2 * core, "head": h}, device_id_type=MESH)

    def tell_heads(sem):
        for d in range(1, n_head):
            pl.semaphore_signal(sem, inc=1, device_id={"seq": s, "head": (h + d) % n_head}, device_id_type=MESH)

    @pl.when(h == 0)
    def _():
        tell_heads(barrier)
    ends = (s < 2).astype(jnp.int32) + (s + 2 >= n_seq).astype(jnp.int32)
    load_k.wait()
    pl.semaphore_wait(barrier, 3 - ends + (h > 0).astype(jnp.int32))

    half = kv // 2

    def win_copy(slot, i):
        part = pl.ds(i * half, half)
        if slot == 0:
            src, to = kt.at[2], s + 2
        else:
            src, to = kt.at[0], s + 1 - 2 * core
        return pltpu.make_async_remote_copy(
            src_ref=src.at[part], dst_ref=kt.at[slot, part], send_sem=wsend.at[2 * slot + i],
            recv_sem=wrecv.at[2 * slot + i], device_id={"seq": to, "head": h}, device_id_type=MESH)

    def own_copy(i):
        part = pl.ds(i * half, half)
        return pltpu.make_async_remote_copy(
            src_ref=kt.at[2, part], dst_ref=kt.at[1, part], send_sem=wsend.at[2 + i],
            recv_sem=wrecv.at[2 + i], device_id={"seq": s + 1, "head": h}, device_id_type=MESH)

    @pl.when(s + 2 < n_seq)
    def _():
        for i in (0, 1):
            win_copy(0, i).start()

    @pl.when(core == 0)
    def _():
        for i in (0, 1):
            own_copy(i).start()

    @pl.when(s < 2)
    def _():
        kt[0] = jnp.zeros((kv, tok), bf16)

    @pl.when(s == 0)
    def _():
        kt[1] = jnp.zeros((kv, tok), bf16)

    @pl.when(s + 2 >= n_seq)
    def _():
        for j in range(N_X):
            rbuf[j] = jnp.zeros((quarter, tok), bf16)

    load_do.start()
    load_q.start()

    @pl.when(h > 0)
    def _():
        pl.semaphore_signal(here, inc=1, device_id={"seq": s, "head": 0}, device_id_type=MESH)

    load_s.wait()
    row = lax.broadcasted_iota(jnp.int32, (tok, tok), 0)
    col = lax.broadcasted_iota(jnp.int32, (tok, tok), 1)
    tri = row <= col
    seg_q = jnp.broadcast_to(seg[pl.ds(s, 1), :], (tok, tok))

    def key_seg(d):
        line = jnp.broadcast_to(seg[pl.ds(jnp.maximum(s - d, 0), 1), :], (tok, tok))
        line = jnp.where(s - d >= 0, line, -1)
        return jnp.transpose(line)

    seen_p = jnp.where(tri, key_seg(0), key_seg(2)) == seg_q
    seen_1 = key_seg(1) == seg_q
    mask[0] = jnp.where(seen_1, 0.0, masked_score)
    mask[1] = jnp.where(seen_p, 0.0, masked_score)

    kk[pl.ds(2 * tok, tok), :] = jnp.transpose(kt[2])
    load_do.wait()
    r = lax.broadcasted_iota(jnp.int32, (256, 256), 0)
    c = lax.broadcasted_iota(jnp.int32, (256, 256), 1)
    perm = ((r // 16 == c % 16) & (r % 16 == c // 16)).astype(bf16)
    for i in range(tok // 16):
        part = dot(perm, do[pl.ds(i * 256, 256), :]).astype(bf16)
        for hh in range(heads):
            doh[pl.ds(hh * tok + i * 16, 16), :] = part[hh * 16:(hh + 1) * 16]
    for hh in range(heads):
        dot_[hh] = jnp.transpose(doh[pl.ds(hh * tok, tok), :])
    load_q.wait()

    def pair(ref, p):
        return jnp.concatenate([ref[2 * p], ref[2 * p + 1]], axis=1)

    for p in range(pairs):
        lanes = pl.ds(p * 256, 256)
        s0[:, lanes] = dot(kk[pl.ds(2 * tok, tok), :], pair(q, p))
        g0[:, lanes] = dot(kk[pl.ds(2 * tok, tok), :LATENT], pair(dot_, p))

    @pl.when(h == 0)
    def _():
        pl.semaphore_wait(here, n_head - 1)
        tell_heads(here)

    for hh in range(heads):
        qn[pl.ds(hh * tok, tok), :] = jnp.transpose(q[hh])

    @pl.when(h > 0)
    def _():
        pl.semaphore_wait(here, 1)

    tri2 = jnp.concatenate([tri, tri], axis=1)
    m1 = jnp.concatenate([mask[0], mask[0]], axis=1)
    mp = jnp.concatenate([mask[1], mask[1]], axis=1)

    def first(slot):
        rows = pl.ds(slot * tok, tok)
        kk[rows, :] = jnp.transpose(kt[slot])
        for p in range(pairs):
            lanes = pl.ds(p * 256, 256)
            sx[:, lanes] = dot(kk[rows, :], pair(q, p))
            gx[:, lanes] = dot(kk[rows, :LATENT], pair(dot_, p))

    def second(slot):
        rows = pl.ds(slot * tok, tok)
        kk[rows, :] = jnp.transpose(kt[slot])
        for p in range(pairs):
            lanes = pl.ds(p * 256, 256)
            sy = dot(kk[rows, :], pair(q, p))
            gy = dot(kk[rows, :LATENT], pair(dot_, p))
            s1, s2 = (sy, sx[:, lanes]) if slot == 1 else (sx[:, lanes], sy)
            g1, g2 = (gy, gx[:, lanes]) if slot == 1 else (gx[:, lanes], gy)
            weigh(lanes, s1, s2, g1, g2)

    def weigh(lanes, s1, s2, g1, g2):
        sp = jnp.where(tri2, s0[:, lanes], s2) + mp
        s1 = s1 + m1
        top = jnp.maximum(jnp.max(sp, axis=0, keepdims=True), jnp.max(s1, axis=0, keepdims=True))
        ep = jnp.exp2((sp - top) * exp2_scale)
        e1 = jnp.exp2((s1 - top) * exp2_scale)
        inv = 1.0 / (jnp.sum(ep, axis=0, keepdims=True) + jnp.sum(e1, axis=0, keepdims=True))
        wp, w1 = ep * inv, e1 * inv
        wlp, wl1 = wp.astype(bf16), w1.astype(bf16)
        gp = jnp.where(tri2, g0[:, lanes], g2)
        delta = (jnp.sum(wlp.astype(f32) * gp, axis=0, keepdims=True)
                 + jnp.sum(wl1.astype(f32) * g1, axis=0, keepdims=True))
        dsp = (score_scale * wp * (gp - delta)).astype(bf16)
        ds1 = (score_scale * w1 * (g1 - delta)).astype(bf16)
        zero = jnp.zeros_like(wlp)
        p_all[tok:2 * tok, lanes] = jnp.where(tri2, zero, wlp)
        p_all[0:tok, lanes] = wl1
        p_all[2 * tok:, lanes] = jnp.where(tri2, wlp, zero)
        ds_all[tok:2 * tok, lanes] = jnp.where(tri2, zero, dsp)
        ds_all[0:tok, lanes] = ds1
        ds_all[2 * tok:, lanes] = jnp.where(tri2, dsp, zero)

    def tell():
        for d in range(1, N_X):
            pl.semaphore_signal(ready, inc=1, device_id={"seq": s, "head": (h + 2 * d) % n_head}, device_id_type=MESH)

    @pl.when(core == 0)
    def _():
        @pl.when(s >= 2)
        def _():
            for i in (0, 1):
                win_copy(0, i).wait_recv()
        tell()
        first(0)

        @pl.when(s >= 2)
        def _():
            for i in (0, 1):
                win_copy(1, i).wait_recv()
        second(1)

    @pl.when(core == 1)
    def _():
        for i in (0, 1):
            win_copy(1, i).wait_recv()
        first(1)

        @pl.when(s >= 2)
        def _():
            for i in (0, 1):
                win_copy(0, i).wait_recv()
                win_copy(1, i).start()
        tell()
        second(0)

    def key_grad(rows):
        from_keys = dot(ds_all[rows, :], qn[...])
        return from_keys[:, :LATENT] + dot(p_all[rows, :], doh[...]), from_keys[:, LATENT:]

    swap = pltpu.make_async_remote_copy(
        src_ref=pmid.at[0], dst_ref=pmid.at[1], send_sem=msem.at[0], recv_sem=msem.at[1],
        device_id={"seq": s + 1 - 2 * core, "head": h}, device_id_type=MESH)

    parts = ((0, 80), (80, quarter - 80))

    def part_copy(b, j, i):
        xx = (x + j) % N_X
        slot = b * N_X + j - b
        begin, size = parts[i]
        return pltpu.make_async_remote_copy(
            src_ref=psend.at[b, pl.ds(pl.multiple_of(xx * quarter + begin, 16), size)],
            dst_ref=rbuf.at[slot, pl.ds(begin, size)], send_sem=psems.at[2 * slot + i],
            recv_sem=precv.at[2 * slot + i],
            device_id={"seq": s - 2 * (1 - b), "head": xx * 2 + y}, device_id_type=MESH)

    low, high = key_grad(pl.ds(0, tok))
    pmid[0, :, :LATENT] = low.astype(bf16)
    pmid[0, :, LATENT:] = high.astype(bf16)

    @pl.when(s > 0)
    def _():
        swap.start()
    low, high = key_grad(pl.ds(tok, 2 * tok))
    pown[:, :LATENT] = low
    pown[:, LATENT:] = high
    pl.semaphore_wait(ready, N_X - 1)

    def emit(b, add):
        rows = pl.ds(b * tok, tok)
        if add:
            swap.wait_recv()
            psend[b] = jnp.transpose((pown[rows, :] + pmid[1].astype(f32)).astype(bf16))
        else:
            psend[b] = jnp.transpose(pown[rows, :].astype(bf16))
        if b == 0:
            @pl.when(s >= 2)
            def _():
                for i in (0, 1):
                    for j in (2, 1, 3, 0):
                        part_copy(0, j, i).start()
        else:
            for i in (0, 1):
                for j in (2, 1, 3):
                    part_copy(1, j, i).start()

    @pl.when(core == 0)
    def _():
        emit(1, True)
        emit(0, False)

    @pl.when(core == 1)
    def _():
        emit(1, False)

    @pl.when((core == 1) & (s >= 2))
    def _():
        emit(0, True)

    ktall = jnp.concatenate([kt[1], kt[0], kt[2]], axis=1)
    for p in range(pairs):
        out = dot(ktall, ds_all[:, pl.ds(p * 256, 256)]).astype(bf16)
        dq[2 * p] = out[:, :tok]
        dq[2 * p + 1] = out[:, tok:]


    def gather_copy(d, i):
        begin, size = parts[i]
        mine = pl.ds(pl.multiple_of(x * quarter + begin, 16), size)
        return pltpu.make_async_remote_copy(
            src_ref=gbuf.at[y, mine], dst_ref=gbuf.at[y, mine],
            send_sem=gsend.at[2 * d - 2 + i], recv_sem=grecv.at[2 * d - 2 + i],
            device_id={"seq": s, "head": (h + d) % n_head}, device_id_type=MESH)

    for i in (0, 1):
        begin, size = parts[i]
        mine = pl.ds(pl.multiple_of(x * quarter + begin, 16), size)
        total = psend[1, mine, :].astype(f32)
        for j in range(1, N_X):
            part_copy(1, j, i).wait_recv()
            total = total + rbuf[N_X + j - 1, begin:begin + size].astype(f32)

        @pl.when(s + 2 < n_seq)
        def _():
            for j in range(N_X):
                part_copy(0, j, i).wait_recv()
        for j in range(N_X):
            total = total + rbuf[j, begin:begin + size].astype(f32)
        gbuf[y, mine, :] = total.astype(bf16)
        for d in (3, 5, 4, 1, 7, 2, 6):
            gather_copy(d, i).start()
    for i in (0, 1):
        for d in (2, 6, 1, 7, 4, 3, 5):
            gather_copy(d, i).wait_recv()
    gc_ref[...] = (gbuf[0].astype(f32) + gbuf[1].astype(f32)).astype(bf16)

    @pl.when(s + 2 < n_seq)
    def _():
        for i in (0, 1):
            win_copy(0, i).wait_send()

    @pl.when((core == 0) | (s >= 2))
    def _():
        for i in (0, 1):
            win_copy(1, i).wait_send()

    @pl.when(s > 0)
    def _():
        swap.wait_send()

    @pl.when(s >= 2)
    def _():
        for j in range(N_X):
            for i in (0, 1):
                part_copy(0, j, i).wait_send()
    for i in (0, 1):
        for j in range(1, N_X):
            part_copy(1, j, i).wait_send()
        for d in range(1, n_head):
            gather_copy(d, i).wait_send()


def store_kernel(dq, gc, dq_hbm, gc_hbm, sems):
    copies = [pltpu.make_async_copy(gc, gc_hbm, sems.at[0]), pltpu.make_async_copy(dq, dq_hbm, sems.at[1])]
    for c in copies:
        c.start()
    for c in copies:
        c.wait()


def local(n_seq, n_head, queries, latent_cache, grad_out, segment_ids):
    tok, heads, kv = queries.shape
    q = jnp.transpose(queries, (1, 2, 0))
    kt = jnp.transpose(latent_cache)
    do = grad_out.reshape(tok * heads, LATENT)
    seg = segment_ids.reshape(n_seq, tok)
    rows = tok * heads
    quarter = kv // N_X
    dma = pltpu.SemaphoreType.DMA
    hbm = pl.BlockSpec(memory_space=pltpu.HBM)
    dq, gc = pl.pallas_call(
        functools.partial(kernel, n_seq, n_head),
        out_shape=(pltpu.VMEM((heads, kv, tok), bf16), pltpu.VMEM((kv, tok), bf16)),
        in_specs=[hbm] * 4,
        out_specs=(pl.BlockSpec(memory_space=pltpu.VMEM), pl.BlockSpec(memory_space=pltpu.VMEM)),
        scratch_shapes=[
            pltpu.VMEM((heads, kv, tok), bf16),
            pltpu.VMEM((3, kv, tok), bf16),
            pltpu.VMEM((3 * tok, kv), bf16),
            pltpu.VMEM((rows, LATENT), bf16),
            pltpu.VMEM((rows, LATENT), bf16),
            pltpu.VMEM((rows, kv), bf16),
            pltpu.VMEM((heads, LATENT, tok), bf16),
            pltpu.VMEM((n_seq, tok), jnp.int32),
            pltpu.VMEM((tok, rows), f32),
            pltpu.VMEM((tok, rows), f32),
            pltpu.VMEM((tok, rows), f32),
            pltpu.VMEM((tok, rows), f32),
            pltpu.VMEM((3 * tok, rows), bf16),
            pltpu.VMEM((3 * tok, rows), bf16),
            pltpu.VMEM((2, tok, tok), f32),
            pltpu.VMEM((2, tok, kv), bf16),
            pltpu.VMEM((2, kv, tok), bf16),
            pltpu.VMEM((2 * tok, kv), f32),
            pltpu.VMEM((2 * N_X - 1, quarter, tok), bf16),
            pltpu.VMEM((2, kv, tok), bf16),
            dma((4,)), dma((4,)), dma((4,)), dma((2,)),
            dma((4 * N_X - 2,)), dma((4 * N_X - 2,)), dma((2 * n_head - 2,)), dma((2 * n_head - 2,)),
            pltpu.SemaphoreType.REGULAR,
            pltpu.SemaphoreType.REGULAR,
        ],
        compiler_params=pltpu.CompilerParams(
            collective_id=0, has_side_effects=True, vmem_limit_bytes=50 << 20),
        cost_estimate=pl.CostEstimate(flops=6 * 10**9, bytes_accessed=8 * 10**6, transcendentals=10**6),
        name="latent_backward",
    )(*[pltpu.with_memory_space_constraint(a, pltpu.HBM) for a in (q, kt, do, seg)])
    dq, gc = pl.pallas_call(
        store_kernel,
        out_shape=(jax.ShapeDtypeStruct((heads, kv, tok), bf16), jax.ShapeDtypeStruct((kv, tok), bf16)),
        in_specs=[pl.BlockSpec(memory_space=pltpu.VMEM)] * 2,
        out_specs=(hbm, hbm),
        scratch_shapes=[dma((2,))],
        name="store",
    )(*[pltpu.with_memory_space_constraint(a, pltpu.VMEM) for a in (dq, gc)])
    return jnp.transpose(dq, (2, 0, 1)), jnp.transpose(gc)


def solution(mesh):
    in_specs = (P("seq", "head", None), P("seq", None), P("seq", "head", None), P())
    out_specs = (P("seq", "head", None), P("seq", None))
    return jax.shard_map(
        functools.partial(local, mesh.shape["seq"], mesh.shape["head"]),
        mesh=mesh, in_specs=in_specs, out_specs=out_specs, check_vma=False)
```
